32 devices in a mesh: dp: 4 (over y, x), row: 2 (over core), col: 4 (over z).
Axes of the slice: x: 2, y: 2, z: 4, core: 2. Of those that a mesh axis runs over, the one named last changes fastest.
Arguments:
- inputs: bfloat16 [6144, 6144], P('dp', 'row'), may hold values from -6 to 6
- pre_act: bfloat16 [6144, 12288], P(('dp', 'row'), 'col'), may hold values from -8 to 8
- out_grad: bfloat16 [6144, 12288], P(('dp', 'row'), 'col'), may hold values from -6 to 6
- weight: bfloat16 [6144, 12288], P('row', 'col'), may hold values from -6 to 6
- swag_mean: float32 [4, 1536, 12288], P('dp', 'row', 'col'), may hold values from -6 to 6
- swag_square: float32 [4, 1536, 12288], P('dp', 'row', 'col'), may hold values from 0.5 to 3
- snapshots: int32 [1], replicated, may hold values from 1 to 32
- update_flag: int32 [4, 1536], P('dp', 'row'), may hold values 0 or 1
Outputs:
- input_grad: bfloat16 [6144, 6144], P(('dp', 'col'), 'row')
- new_weight: float32 [4, 1536, 12288], P('dp', 'row', 'col')
- mean_out: float32 [4, 1536, 12288], P('dp', 'row', 'col')
- square_out: float32 [4, 1536, 12288], P('dp', 'row', 'col')
The draws below stay inside these ranges and needn't reach their ends.
All inputs are finite; a program needn't handle non-finite values. No bound on the sum of `update_flag` on one device may be relied on, other than what follows from the above.
Results may differ from the reference program's by a relative error of at most 0.013.
Values may be sent and summed in bfloat16 or wider, within the bound.
No kernel may reach another device: no remote copies, remote signals or barrier semaphores. Data moves between devices by JAX's collectives and lax.ppermute only.
A program may use at most 192 MiB of HBM per device.

```python
import jax
import jax.numpy as jnp
from jax import lax

D = 6144
FF = 12288
TOK = 1536
TOKENS = 6144
SHARE = 768
N_DP = 4
N_ROW = 2
N_COL = 4


def place_ends(result, rng, smallest, largest):
    place = [jax.random.randint(jax.random.fold_in(rng, axis), (), 0, length) for axis, length in enumerate(result.shape)]
    widest = result.shape.index(max(result.shape))
    next_to = place[:widest] + [(place[widest] + 1) % result.shape[widest]] + place[widest + 1:]
    return result.at[tuple(place)].set(smallest).at[tuple(next_to)].set(largest)


def block_levels(rng, extent, split, smallest, high):
    loudness = 1.0
    for position, shards_of in split:
        heights = jax.random.uniform(jax.random.fold_in(jax.random.fold_in(rng, 6), position), (shards_of,), jnp.float32, smallest / len(split), high / len(split))
        loudness = loudness * jnp.repeat(jnp.exp(heights), extent[position] // shards_of).reshape((-1,) + (1,) * (len(extent) - 1 - position))
    return loudness


def normal_values(rng, dims, deviation, most, cuts=(), held_as=jnp.bfloat16):
    result = jax.random.normal(rng, dims, jnp.float32) * deviation
    if len(cuts) > 0:
        result = block_levels(rng, dims, cuts, -0.22, 0.18) * result
    return jnp.clip(result, min=-most, max=most).astype(held_as)


def setup_inputs(seed: int = 0) -> dict:
    keys = jax.random.split(jax.random.key(seed), 9)
    inputs = normal_values(keys[0], (TOKENS, D), 1.0, 6.0, ((0, 4), (1, 2)))
    pre_act = normal_values(keys[1], (TOKENS, FF), 1.5, 8.0, ((0, 8), (1, 4)))
    out_grad = normal_values(keys[2], (TOKENS, FF), 1.0, 6.0, ((0, 8), (1, 4)))
    weight = normal_values(keys[3], (D, FF), 1.0, 6.0, ((0, 2), (1, 4)))
    swag_mean = normal_values(keys[4], (N_DP, D // N_DP, FF), 1.0, 6.0, ((0, 4), (1, 2), (2, 4)), jnp.float32)
    swag_square = jnp.clip(0.5 + 2.5 * jax.random.uniform(keys[5], (N_DP, D // N_DP, FF), jnp.float32) ** block_levels(keys[5], (N_DP, D // N_DP, FF), ((0, 4), (1, 2), (2, 4)), -0.2, 0.2), 0.5, 3.0)
    snapshots = jax.random.randint(keys[6], (1,), 1, 33).astype(jnp.int32)
    update_flag = place_ends((jax.random.randint(keys[7], (N_DP, D // N_DP), 0, 2) < 1).astype(jnp.int32), jax.random.fold_in(keys[7], 1), 0, 1)
    return dict(inputs=inputs, pre_act=pre_act, out_grad=out_grad, weight=weight, swag_mean=swag_mean, swag_square=swag_square, snapshots=snapshots, update_flag=update_flag)


learning_rate = 0.5


def gelu_slope(values):
    normal_cdf = 0.5 * (1.0 + lax.erf(values * 0.7071067811865476))
    density = jnp.exp(-0.5 * values * values) * 0.3989422804014327
    return normal_cdf + values * density


def rounded(values):
    return lax.optimization_barrier(values.astype(jnp.bfloat16)).astype(jnp.float32)


def reference(inputs, pre_act, out_grad, weight, swag_mean, swag_square, snapshots, update_flag):
    multiplier = 1.0 / (D ** 0.5)
    pre_grad = (out_grad.astype(jnp.float32) * gelu_slope(pre_act.astype(jnp.float32))).astype(jnp.bfloat16)
    block_cols = FF // N_COL
    total = jnp.zeros((TOKENS, D), jnp.float32)
    for block in range(N_COL):
        grad_block = pre_grad[:, block * block_cols:(block + 1) * block_cols]
        weight_block = weight[:, block * block_cols:(block + 1) * block_cols]
        product = lax.dot_general(grad_block, weight_block, (((1,), (1,)), ((), ())), preferred_element_type=jnp.float32)
        total = total + rounded(product * multiplier)
    input_grad = total.astype(jnp.bfloat16)
    summed = jnp.zeros((D, FF), jnp.float32)
    for replica in range(N_DP):
        input_rows = inputs[replica * TOK:(replica + 1) * TOK]
        grad_rows = pre_grad[replica * TOK:(replica + 1) * TOK]
        product = lax.dot_general(input_rows, grad_rows, (((0,), (0,)), ((), ())), preferred_element_type=jnp.float32)
        summed = summed + rounded(product)
    stepped = weight.astype(jnp.float32) - learning_rate * (summed / (TOKENS ** 0.5))
    regrouped = stepped.reshape(N_ROW, N_DP, SHARE, FF).transpose(1, 0, 2, 3).reshape(N_DP, D // N_DP, FF)
    blend = update_flag.astype(jnp.float32)[:, :, None] / (snapshots[0].astype(jnp.float32) + 1.0)
    mean_out = swag_mean + blend * (regrouped - swag_mean)
    square_out = swag_square + blend * (regrouped * regrouped - swag_square)
    return input_grad, regrouped, mean_out, square_out
```

```python
import jax
import jax.numpy as jnp
from jax import lax
from jax.experimental import pallas as pl
from jax.experimental.pallas import tpu as pltpu
from jax.sharding import PartitionSpec as P

D = 6144


learning_rate = 0.5
VMEM_LIMIT = 56 * 1024 * 1024
LANES = 128
TOKEN = (8, LANES)


def gelu_slope(values):
    normal_cdf = 0.5 * (1.0 + lax.erf(values * 0.7071067811865476))
    density = jnp.exp(-0.5 * values * values) * 0.3989422804014327
    return normal_cdf + values * density


def times_slope(out_grad, pre_act):
    return (out_grad.astype(jnp.float32) * gelu_slope(pre_act.astype(jnp.float32))).astype(jnp.bfloat16)


def dot(a, b, dims):
    return lax.dot_general(a, b, (dims, ((), ())), preferred_element_type=jnp.float32)


def params():
    return pltpu.CompilerParams(dimension_semantics=("arbitrary",), vmem_limit_bytes=VMEM_LIMIT)


def anywhere(arrays):
    return [pl.BlockSpec(memory_space=pl.ANY)] * len(arrays)


def block_width(width, most):
    return max(b for b in range(LANES, min(width, most) + 1, LANES) if width % b == 0)


def weight_product(inputs, local, remote, ids, share, start, width, deps=(), add=None):
    half = local.shape[0]
    bn = block_width(width, 512)
    first = start // bn

    def kernel(ids_ref, a0, a1, g0, g1, *rest):
        more, (out, token, t0, t1) = rest[: -4], rest[-4:]

        @pl.when(pl.program_id(0) == 0)
        def _():
            t0[...] = a0[...].T
            t1[...] = a1[...].T
            token[...] = jnp.zeros_like(token)

        acc = dot(t0[...], g0[...], ((1,), (0,))) + dot(t1[...], g1[...], ((1,), (0,)))
        if add is not None:
            acc = acc + more[0][...].astype(jnp.float32)
        out[...] = acc.astype(out.dtype)

    extra = [] if add is None else [add]
    return pl.pallas_call(
        kernel,
        grid_spec=pltpu.PrefetchScalarGridSpec(
            num_scalar_prefetch=1,
            grid=(width // bn,),
            in_specs=[
                pl.BlockSpec((half, share), lambda j, ids: (ids[1], ids[0])),
                pl.BlockSpec((half, share), lambda j, ids: (ids[2], ids[0])),
                pl.BlockSpec((half, bn), lambda j, ids: (0, first + j)),
                pl.BlockSpec((half, bn), lambda j, ids: (0, first + j)),
            ]
            + [pl.BlockSpec((share, bn), lambda j, ids: (0, j))] * len(extra)
            + anywhere(deps),
            out_specs=[
                pl.BlockSpec((share, bn), lambda j, ids: (0, j)),
                pl.BlockSpec(TOKEN, lambda j, ids: (0, 0)),
            ],
            scratch_shapes=[pltpu.VMEM((share, half), jnp.bfloat16)] * 2,
        ),
        out_shape=[jax.ShapeDtypeStruct((share, width), jnp.bfloat16), jax.ShapeDtypeStruct(TOKEN, jnp.float32)],
        compiler_params=params(),
        cost_estimate=pl.CostEstimate(
            flops=4 * half * share * width,
            bytes_accessed=2 * (2 * half * (share + width) + share * width * (1 + len(extra))),
            transcendentals=0,
        ),
        name="weight_product",
    )(ids, inputs, inputs, local, remote, *extra, *deps)


def input_product(weight, locals_, remotes, ids, rows, multiplier, deps=()):
    width, hidden = weight.shape
    bn = block_width(width, 512)
    count = len(locals_)

    def kernel(ids_ref, w, *rest):
        mine, others = rest[:count], rest[count : 2 * count]
        out, token, lhs = rest[-3:]

        @pl.when(pl.program_id(0) == 0)
        def _():
            token[...] = jnp.zeros_like(token)

        for chosen, refs in ((1, mine), (0, others)):

            @pl.when((pl.program_id(0) == 0) & (ids_ref[1] == chosen))
            def _():
                at = 0
                for ref in refs:
                    lhs[:, at : at + ref.shape[1]] = ref[...]
                    at += ref.shape[1]

        out[...] = (dot(lhs[...], w[...], ((1,), (1,))) * multiplier).astype(out.dtype)

    return pl.pallas_call(
        kernel,
        grid_spec=pltpu.PrefetchScalarGridSpec(
            num_scalar_prefetch=1,
            grid=(width // bn,),
            in_specs=[pl.BlockSpec((bn, hidden), lambda j, ids: (j, 0))]
            + [pl.BlockSpec((rows, a.shape[1]), lambda j, ids: (ids[0], 0)) for a in (*locals_, *remotes)]
            + anywhere(deps),
            out_specs=[
                pl.BlockSpec((rows, bn), lambda j, ids: (0, j)),
                pl.BlockSpec(TOKEN, lambda j, ids: (0, 0)),
            ],
            scratch_shapes=[pltpu.VMEM((rows, hidden), jnp.bfloat16)],
        ),
        out_shape=[jax.ShapeDtypeStruct((rows, width), jnp.bfloat16), jax.ShapeDtypeStruct(TOKEN, jnp.float32)],
        compiler_params=params(),
        cost_estimate=pl.CostEstimate(
            flops=2 * rows * width * hidden,
            bytes_accessed=2 * (width * hidden + 2 * rows * hidden + rows * width),
            transcendentals=0,
        ),
        name="input_product",
    )(ids, weight, *locals_, *remotes, *deps)


def update(inputs, local, remote, ids, received, weight, mean, square, blend, start, offset, width, scale, before):
    half = local.shape[0]
    share = mean.shape[1]
    bn = block_width(width, 256)
    first, place = start // bn, (offset + start) // bn
    terms = len(received)
    shape = jax.ShapeDtypeStruct(mean.shape, jnp.float32)

    def kernel(ids_ref, a0, a1, g0, g1, w, m, s, b, *rest):
        others = rest[:terms]
        new_w, new_m, new_s, t0, t1 = rest[-5:]

        @pl.when(pl.program_id(0) == 0)
        def _():
            t0[...] = a0[...].T
            t1[...] = a1[...].T

        total = dot(t0[...], g0[...], ((1,), (0,))) + dot(t1[...], g1[...], ((1,), (0,)))
        for other in others:
            total = total + other[...].astype(jnp.float32)
        stepped = w[...].astype(jnp.float32) - scale * total
        new_w[0] = stepped
        new_m[0] = m[0] + b[...] * (stepped - m[0])
        new_s[0] = s[0] + b[...] * (stepped * stepped - s[0])

    moment = pl.BlockSpec((1, share, bn), lambda j, ids: (0, 0, place + j))
    n_in = 9 + terms
    return pl.pallas_call(
        kernel,
        grid_spec=pltpu.PrefetchScalarGridSpec(
            num_scalar_prefetch=1,
            grid=(width // bn,),
            in_specs=[
                pl.BlockSpec((half, share), lambda j, ids: (ids[1], ids[0])),
                pl.BlockSpec((half, share), lambda j, ids: (ids[2], ids[0])),
                pl.BlockSpec((half, bn), lambda j, ids: (0, first + j)),
                pl.BlockSpec((half, bn), lambda j, ids: (0, first + j)),
                pl.BlockSpec((share, bn), lambda j, ids: (ids[0], place + j)),
                moment,
                moment,
                pl.BlockSpec((share, 1), lambda j, ids: (0, 0)),
            ]
            + [pl.BlockSpec((share, bn), lambda j, ids: (0, j))] * terms
            + anywhere(before),
            out_specs=[moment] * 3,
            scratch_shapes=[pltpu.VMEM((share, half), jnp.bfloat16)] * 2,
        ),
        out_shape=[shape] * 3,
        input_output_aliases={n_in + k: k for k in range(len(before))},
        compiler_params=params(),
        cost_estimate=pl.CostEstimate(
            flops=4 * half * share * width,
            bytes_accessed=2 * 2 * half * (share + width) + share * width * (2 + 8 + 12 + 2 * terms),
            transcendentals=0,
        ),
        name="update",
    )(ids, inputs, inputs, local, remote, weight, mean, square, blend, *received, *before)


def plain_body(inputs, pre_act, out_grad, weight, swag_mean, swag_square, snapshots, update_flag):
    row_width = weight.shape[0]
    groups = lax.axis_size("dp")
    share_rows = row_width // groups
    multiplier = 1.0 / D**0.5
    local_grad = times_slope(out_grad, pre_act)
    portion = lax.all_gather(local_grad, "row", axis=0, tiled=True)
    grad_acc = dot(inputs, portion, ((0,), (0,)))
    term_rows = dot(portion, weight, ((1,), (1,))) * multiplier
    input_grad = lax.psum_scatter(term_rows.astype(jnp.bfloat16), "col", scatter_dimension=0, tiled=True)
    share = lax.psum_scatter(grad_acc.astype(jnp.bfloat16), "dp", scatter_dimension=0, tiled=True).astype(jnp.float32)
    own_rows = lax.dynamic_slice_in_dim(weight, lax.axis_index("dp") * share_rows, share_rows, 0).astype(jnp.float32)
    total_tokens = inputs.shape[0] * groups
    stepped = own_rows - learning_rate * (share / total_tokens**0.5)
    blend = update_flag[0].astype(jnp.float32)[:, None] / (snapshots[0].astype(jnp.float32) + 1.0)
    mean_new = swag_mean[0] + blend * (stepped - swag_mean[0])
    square_new = swag_square[0] + blend * (stepped * stepped - swag_square[0])
    return (input_grad, stepped[None], mean_new[None], square_new[None])


def body(inputs, pre_act, out_grad, weight, swag_mean, swag_square, snapshots, update_flag):
    tokens = inputs.shape[0]
    half = pre_act.shape[0]
    width, hidden = weight.shape
    groups, cols = lax.axis_size("dp"), lax.axis_size("col")
    share = width // groups
    rows = tokens // cols
    multiplier = 1.0 / D**0.5
    scale = learning_rate / (tokens * groups) ** 0.5
    me, core, place = lax.axis_index("dp"), lax.axis_index("row"), lax.axis_index("col")

    def swap(value, axis, bit):
        return lax.ppermute(value, axis, [(i, i ^ bit) for i in range(lax.axis_size(axis))])

    piece = hidden // 2
    starts = (0, piece)
    mine = [times_slope(out_grad[:, s : s + piece], pre_act[:, s : s + piece]) for s in starts]
    theirs = [swap(value, "row", 1) for value in mine]
    blend = update_flag[0].astype(jnp.float32)[:, None] / (snapshots[0].astype(jnp.float32) + 1.0)

    def product(index, k, deps, add=None):
        ids = jnp.stack([index, core, 1 - core]).astype(jnp.int32)
        out, token = weight_product(inputs, mine[k], theirs[k], ids, share, 0, piece, deps, add)
        return out, [token]

    turns = []
    for i in range(cols):
        if 2 * i < cols:
            order = [c for c in range(cols - 1, i, -1)] + [c for c in range(i)] + [i]
        else:
            order = [c for c in range(i)] + [c for c in range(cols - 1, i, -1)] + [i]
        turns.append(order)
    turns = jnp.array(turns, jnp.int32)
    per_half = half // rows

    def chunk(turn, deps):
        index = turns[place, turn]
        ids = jnp.stack([index % per_half, (index // per_half == core).astype(jnp.int32)]).astype(jnp.int32)
        out, token = input_product(weight, mine, theirs, ids, rows, multiplier, deps)
        return out, [token]

    near = (1, 2)
    far = (2, 1)
    outer = ((0, 1), (cols - 1, cols - 2))
    middle = ((1, 2), (2, 1))
    inner = ((1, 0), (cols - 2, cols - 1))

    def along(value, pairs):
        return lax.ppermute(value, "col", pairs)

    def plus(*values):
        return sum(v.astype(jnp.float32) for v in values).astype(jnp.bfloat16)

    pass_a, order = product(me ^ 3, 0, [])
    got_pass_a = swap(pass_a, "dp", near[0])
    pass_b, order = product(me ^ 3, 1, order)
    got_pass_b = swap(pass_b, "dp", near[1])
    c0, order = chunk(0, order)
    got_o0 = along(c0, outer)
    keep_a, order = product(me ^ near[0], 0, order)
    got_keep_a = swap(keep_a, "dp", near[0])
    keep_b, order = product(me ^ near[1], 1, order)
    got_keep_b = swap(keep_b, "dp", near[1])
    c1, order = chunk(1, order)
    got_o1 = along(c1, outer)
    c2, order = chunk(2, order)
    got_o2 = along(c2, outer)
    c3, order = chunk(3, order)
    got_m1 = along(plus(c0, got_o0), middle)
    last_a, order = product(me ^ far[0], 0, order, got_pass_a)
    got_last_a = swap(last_a, "dp", far[0])
    last_b, order = product(me ^ far[1], 1, order, got_pass_b)
    got_last_b = swap(last_b, "dp", far[1])
    got_m2 = along(plus(c1, got_o1), middle)
    got_i = along(plus(c2, got_m1), inner)

    ids = jnp.stack([me, core, 1 - core]).astype(jnp.int32)
    outs = ()
    for k, got in ((0, (got_keep_a, got_last_a)), (1, (got_keep_b, got_last_b))):
        outs = update(
            inputs, mine[k], theirs[k], ids, got, weight, swag_mean, swag_square, blend, 0, starts[k], piece, scale, outs
        )
    input_grad = plus(c3, got_o2, got_m2, got_i)
    return (input_grad, *outs)


def solution(mesh):
    in_specs = (
        P("dp", "row"),
        P(("dp", "row"), "col"),
        P(("dp", "row"), "col"),
        P("row", "col"),
        P("dp", "row", "col"),
        P("dp", "row", "col"),
        P(),
        P("dp", "row"),
    )
    out_specs = (
        P(("dp", "col"), "row"),
        P("dp", "row", "col"),
        P("dp", "row", "col"),
        P("dp", "row", "col"),
    )
    scheduled = dict(mesh.shape) == {"dp": 4, "row": 2, "col": 4}
    return jax.shard_map(
        body if scheduled else plain_body, mesh=mesh, in_specs=in_specs, out_specs=out_specs, check_vma=False
    )
```

```python
import jax
import jax.numpy as jnp
from jax import lax
from jax.experimental import pallas as pl
from jax.experimental.pallas import tpu as pltpu
from jax.sharding import PartitionSpec as P

D = 6144


learning_rate = 0.5
VMEM_LIMIT = 24 * 1024 * 1024
LANES = 128
TOKEN = (8, LANES)
HINT = 20


def gelu_slope(values):
    normal_cdf = 0.5 * (1.0 + lax.erf(values * 0.7071067811865476))
    density = jnp.exp(-0.5 * values * values) * 0.3989422804014327
    return normal_cdf + values * density


def times_slope(out_grad, pre_act):
    return (out_grad.astype(jnp.float32) * gelu_slope(pre_act.astype(jnp.float32))).astype(jnp.bfloat16)


def dot(a, b, dims):
    return lax.dot_general(a, b, (dims, ((), ())), preferred_element_type=jnp.float32)


def params():
    return pltpu.CompilerParams(dimension_semantics=("arbitrary",), vmem_limit_bytes=VMEM_LIMIT)


def anywhere(arrays):
    return [pl.BlockSpec(memory_space=pl.ANY)] * len(arrays)


def block_width(width, most):
    return max(b for b in range(LANES, min(width, most) + 1, LANES) if width % b == 0)


def block_rows(rows, most):
    return max(b for b in range(16, min(rows, most) + 1, 16) if rows % b == 0)


def cost(flops, bytes_accessed):
    return pl.CostEstimate(flops=flops // HINT, bytes_accessed=bytes_accessed // HINT, transcendentals=0)


def held(array):
    return pltpu.with_memory_space_constraint(array, pltpu.HBM)


def clipped(first, count):
    return lambda j, ids: (0, jnp.clip(j - first, 0, count - 1))


def weight_product(inputs, mine, theirs, ids, share, bn, jobs, order, base=None):
    half = mine[0].shape[0]
    begins, steps = [], 0
    for job in jobs:
        begins.append(steps)
        steps += sum(job[4])
    kind = jnp.bfloat16 if base is None else jnp.float32

    def bits_at(j):
        bits = jobs[0][0]
        for begin, job in zip(begins[1:], jobs[1:]):
            bits = jnp.where(j >= begin, job[0], bits)
        return bits

    operands = [inputs, inputs]
    in_specs = [
        pl.BlockSpec((half, share), lambda j, ids: (ids[1], ids[0] ^ bits_at(j))),
        pl.BlockSpec((half, share), lambda j, ids: (1 - ids[1], ids[0] ^ bits_at(j))),
    ]
    out_specs, out_shape, plans = [], [], []
    for begin, (_, piece, first, received, outs) in zip(begins, jobs):
        count = sum(outs)

        def column(j, ids, begin=begin, first=first, count=count):
            return (0, first + jnp.clip(j - begin, 0, count - 1))

        grads = (len(operands), len(operands) + 1)
        operands += [mine[piece], theirs[piece]]
        in_specs += [pl.BlockSpec((half, bn), column)] * 2
        adds, at = [], begin
        for blocks, array in received:
            adds.append((at, at + blocks, len(operands)))
            operands.append(array)
            in_specs.append(pl.BlockSpec((share, bn), clipped(at, blocks)))
            at += blocks
        old = None
        if base is not None:
            old = len(operands)
            operands.append(held(base[0]))
            place = sum(m.shape[1] for m in mine[:piece]) // bn + first
            in_specs.append(
                pl.BlockSpec(
                    (share, bn),
                    lambda j, ids, begin=begin, place=place, count=count: (ids[0], place + jnp.clip(j - begin, 0, count - 1)),
                )
            )
        written, at = [], begin
        for blocks in outs:
            written.append((at, at + blocks, len(out_specs)))
            out_specs.append(pl.BlockSpec((share, bn), clipped(at, blocks)))
            out_shape.append(jax.ShapeDtypeStruct((share, blocks * bn), kind))
            at += blocks
        plans.append((begin, begin + count, grads, adds, old, written))

    def kernel(ids_ref, *refs):
        outs, token = refs[-1 - len(out_specs) : -1], refs[-1]
        step = pl.program_id(0)
        token[...] = jnp.zeros_like(token)
        for begin, end, grads, adds, old, written in plans:

            @pl.when((step >= begin) & (step < end))
            def _():
                result = sum(dot(refs[k][...], refs[g][...], ((0,), (0,))) for k, g in enumerate(grads))
                if adds:
                    more = refs[adds[0][2]][...]
                    for since, _, index in adds[1:]:
                        more = jnp.where(step >= since, refs[index][...], more)
                    result = result + more.astype(jnp.float32)
                if old is not None:
                    result = refs[old][...].astype(jnp.float32) - base[1] * result
                for since, until, index in written:

                    @pl.when((step >= since) & (step < until))
                    def _():
                        outs[index][...] = result.astype(kind)

    *arrays, token = pl.pallas_call(
        kernel,
        grid_spec=pltpu.PrefetchScalarGridSpec(
            num_scalar_prefetch=1,
            grid=(steps,),
            in_specs=in_specs + anywhere(order),
            out_specs=out_specs + [pl.BlockSpec(TOKEN, lambda j, ids: (0, 0))],
        ),
        out_shape=out_shape + [jax.ShapeDtypeStruct(TOKEN, jnp.float32)],
        compiler_params=params(),
        cost_estimate=cost(4 * half * share * bn * steps, 2 * steps * bn * (2 * half + share)),
        name="weight_product",
    )(ids, *operands, *order)
    order[:] = [token]
    return arrays


def chunk_of(turn, place, places):
    above = jnp.where(turn < places - 1 - place, places - 1 - turn, turn - (places - 1 - place))
    below = jnp.where(turn < place, turn, places - 1 - (turn - place))
    return jnp.where(turn == places - 1, place, jnp.where(2 * place < places, above, below))


def input_product(weight, mine, theirs, ids, turns, places, first, wide, multiplier, order):
    hidden = weight.shape[1]
    per_half = places // 2
    rows = mine[0].shape[0] // per_half
    bn = block_width(wide, 512)
    steps = wide // bn
    count = len(mine)

    def kernel(ids_ref, w, *rest):
        own, other = rest[:count], rest[count : 2 * count]
        (token, lhs, sem), outs = rest[-3:], rest[-3 - len(turns) : -3]

        @pl.when(pl.program_id(0) == 0)
        def _():
            token[...] = jnp.zeros_like(token)
            copies = []
            for k, turn in enumerate(turns):
                chunk = chunk_of(turn, ids_ref[2], places)
                here = chunk // per_half == ids_ref[1]
                at = 0
                for g in range(count):
                    columns = own[g].shape[1]
                    rows_at = pl.ds(pl.multiple_of((chunk % per_half) * rows, rows), rows)
                    target = lhs.at[pl.ds(k * rows, rows), pl.ds(at, columns)]
                    near = pltpu.make_async_copy(own[g].at[rows_at, :], target, sem.at[k, g])
                    far = pltpu.make_async_copy(other[g].at[rows_at, :], target, sem.at[k, g])
                    pl.when(here)(near.start)
                    pl.when(jnp.logical_not(here))(far.start)
                    copies.append(near)
                    at += columns
            for copy in copies:
                copy.wait()

        result = (dot(lhs[...], w[...], ((1,), (1,))) * multiplier).astype(jnp.bfloat16)
        for k, out in enumerate(outs):
            out[...] = result[k * rows : (k + 1) * rows]

    *arrays, token = pl.pallas_call(
        kernel,
        grid_spec=pltpu.PrefetchScalarGridSpec(
            num_scalar_prefetch=1,
            grid=(steps,),
            in_specs=[pl.BlockSpec((bn, hidden), lambda j, ids: (first // bn + j, 0))]
            + anywhere(mine)
            + anywhere(theirs)
            + anywhere(order),
            out_specs=[pl.BlockSpec((rows, bn), lambda j, ids: (0, j))] * len(turns)
            + [pl.BlockSpec(TOKEN, lambda j, ids: (0, 0))],
            scratch_shapes=[
                pltpu.VMEM((len(turns) * rows, hidden), jnp.bfloat16),
                pltpu.SemaphoreType.DMA((len(turns), count)),
            ],
        ),
        out_shape=[jax.ShapeDtypeStruct((rows, wide), jnp.bfloat16)] * len(turns)
        + [jax.ShapeDtypeStruct(TOKEN, jnp.float32)],
        compiler_params=params(),
        cost_estimate=cost(
            2 * len(turns) * rows * wide * hidden, 2 * (wide * hidden + len(turns) * rows * (hidden + wide))
        ),
        name="input_product",
    )(ids, held(weight), *mine, *theirs, *order)
    order[:] = [token]
    return arrays


def update(base, last, mean, square, blend, column, bn, scale, before, order):
    share, width = base.shape
    rows = block_rows(share, 256)
    across, place = width // bn, column // bn

    def kernel(old, arrived, m, s, b, *rest):
        new_w, new_m, new_s, token = rest[-4:]
        token[...] = jnp.zeros_like(token)
        stepped = old[...] - scale * arrived[...].astype(jnp.float32)
        new_w[0] = stepped
        new_m[0] = m[0] + b[...] * (stepped - m[0])
        new_s[0] = s[0] + b[...] * (stepped * stepped - s[0])

    moment = pl.BlockSpec((1, rows, bn), lambda i: (0, i // across, place + i % across))
    block = pl.BlockSpec((rows, bn), lambda i: (i // across, i % across))
    *outs, token = pl.pallas_call(
        kernel,
        grid=(share // rows * across,),
        in_specs=[block, block, moment, moment, pl.BlockSpec((rows, 1), lambda i: (i // across, 0))]
        + anywhere(before)
        + anywhere(order),
        out_specs=[moment] * 3 + [pl.BlockSpec(TOKEN, lambda i: (0, 0))],
        out_shape=[jax.ShapeDtypeStruct(mean.shape, jnp.float32)] * 3 + [jax.ShapeDtypeStruct(TOKEN, jnp.float32)],
        input_output_aliases={5 + k: k for k in range(len(before))},
        compiler_params=params(),
        cost_estimate=cost(10 * share * width, share * width * 26),
        name="update",
    )(base, last, held(mean), held(square), blend, *before, *order)
    order[:] = [token]
    return outs


def plain_body(inputs, pre_act, out_grad, weight, swag_mean, swag_square, snapshots, update_flag):
    row_width = weight.shape[0]
    groups = lax.axis_size("dp")
    share_rows = row_width // groups
    multiplier = 1.0 / D**0.5
    local_grad = times_slope(out_grad, pre_act)
    portion = lax.all_gather(local_grad, "row", axis=0, tiled=True)
    grad_acc = dot(inputs, portion, ((0,), (0,)))
    term_rows = dot(portion, weight, ((1,), (1,))) * multiplier
    input_grad = lax.psum_scatter(term_rows.astype(jnp.bfloat16), "col", scatter_dimension=0, tiled=True)
    share = lax.psum_scatter(grad_acc.astype(jnp.bfloat16), "dp", scatter_dimension=0, tiled=True).astype(jnp.float32)
    own_rows = lax.dynamic_slice_in_dim(weight, lax.axis_index("dp") * share_rows, share_rows, 0).astype(jnp.float32)
    total_tokens = inputs.shape[0] * groups
    stepped = own_rows - learning_rate * (share / total_tokens**0.5)
    blend = update_flag[0].astype(jnp.float32)[:, None] / (snapshots[0].astype(jnp.float32) + 1.0)
    mean_new = swag_mean[0] + blend * (stepped - swag_mean[0])
    square_new = swag_square[0] + blend * (stepped * stepped - swag_square[0])
    return (input_grad, stepped[None], mean_new[None], square_new[None])


def plus(terms, order):
    rows, width = terms[0].shape
    some = block_rows(rows, 192)

    def kernel(*refs):
        out, token = refs[-2:]
        token[...] = jnp.zeros_like(token)
        out[...] = sum(ref[...].astype(jnp.float32) for ref in refs[: len(terms)]).astype(out.dtype)

    block = pl.BlockSpec((some, width), lambda i: (i, 0))
    out, token = pl.pallas_call(
        kernel,
        grid=(rows // some,),
        in_specs=[block] * len(terms) + anywhere(order),
        out_specs=[block, pl.BlockSpec(TOKEN, lambda i: (0, 0))],
        out_shape=[jax.ShapeDtypeStruct((rows, width), jnp.bfloat16), jax.ShapeDtypeStruct(TOKEN, jnp.float32)],
        compiler_params=params(),
        cost_estimate=cost(rows * width * len(terms), 2 * rows * width * (len(terms) + 1)),
        name="plus",
    )(*terms, *order)
    order[:] = [token]
    return out


def plus_side_by_side(groups, order):
    rows, width = groups[0][0].shape
    some = block_rows(rows, 96)
    sizes = [len(group) for group in groups]

    def kernel(*refs):
        out, at = refs[-1], 0
        for k, size in enumerate(sizes):
            total = sum(ref[...].astype(jnp.float32) for ref in refs[at : at + size])
            out[:, k * width : (k + 1) * width] = total.astype(out.dtype)
            at += size

    return pl.pallas_call(
        kernel,
        grid=(rows // some,),
        in_specs=[pl.BlockSpec((some, width), lambda i: (i, 0))] * sum(sizes) + anywhere(order),
        out_specs=pl.BlockSpec((some, width * len(groups)), lambda i: (i, 0)),
        out_shape=jax.ShapeDtypeStruct((rows, width * len(groups)), jnp.bfloat16),
        compiler_params=params(),
        cost_estimate=cost(rows * width * sum(sizes), 2 * rows * width * (sum(sizes) + len(groups))),
        name="plus_side_by_side",
    )(*(a for group in groups for a in group), *order)


def body(inputs, pre_act, out_grad, weight, swag_mean, swag_square, snapshots, update_flag):
    tokens = inputs.shape[0]
    half = pre_act.shape[0]
    width, hidden = weight.shape
    groups, cols = lax.axis_size("dp"), lax.axis_size("col")
    share = width // groups
    multiplier = 1.0 / D**0.5
    scale = learning_rate / (tokens * groups) ** 0.5
    ids = jnp.stack([lax.axis_index(axis) for axis in ("dp", "row", "col")]).astype(jnp.int32)

    def swap(value, axis, bit):
        return lax.ppermute(value, axis, [(i, i ^ bit) for i in range(lax.axis_size(axis))])

    piece = hidden // 2
    first = times_slope(out_grad[:, :piece], pre_act[:, :piece])
    rest = lax.optimization_barrier((out_grad, pre_act, first))
    second = times_slope(rest[0][:, piece:], rest[1][:, piece:])
    mine = [first, second]
    theirs = [swap(value, "row", 1) for value in mine]
    blend = update_flag[0].astype(jnp.float32)[:, None] / (snapshots[0].astype(jnp.float32) + 1.0)

    order = []
    bn = block_width(piece, 512)
    blocks = piece // bn
    small = max(1, blocks // 3)
    large = blocks - small

    def products(*jobs, base=None):
        return weight_product(inputs, mine, theirs, ids, share, bn, jobs, order, base)

    parts = 2
    part = width // parts

    def chunks(turns, k):
        return input_product(weight, mine, theirs, ids, turns, cols, k * part, part, multiplier, order)

    near, far = (1, 2), (2, 1)
    middle = ((1, 2), (2, 1))

    def outer(value):
        return swap(value, "col", 1)

    def across(value):
        return lax.ppermute(value, "col", middle)

    (pass_a0,) = products((3, 0, 0, [], [small]))
    got_pass_a0 = swap(pass_a0, "dp", near[0])
    (pass_b0,) = products((3, 1, 0, [], [small]))
    got_pass_b0 = swap(pass_b0, "dp", near[1])
    (c0_a,) = chunks([0], 0)
    got_0a = outer(c0_a)
    pass_a1, pass_b1 = products((3, 0, small, [], [large]), (3, 1, small, [], [large]))
    got_pass_a1, got_pass_b1 = swap(pass_a1, "dp", near[0]), swap(pass_b1, "dp", near[1])
    c0_b, c1_b = chunks([0, 1], 1)
    got_0b, got_1b = outer(c0_b), outer(c1_b)
    keep_a, keep_b = products((near[0], 0, 0, [], [blocks]), (near[1], 1, 0, [], [blocks]))
    got_keep_a, got_keep_b = swap(keep_a, "dp", near[0]), swap(keep_b, "dp", near[1])
    order += [got_pass_a0, got_pass_b0]
    got_m1a = across(plus([c0_a, got_0a], order))
    c1_a, c2_a, c3_a = chunks([1, 2, 3], 0)
    got_1a = outer(c1_a)
    order += [got_pass_a1, got_pass_b1]
    got_m1b = across(plus([c0_b, got_0b], order))
    c2_b, c3_b = chunks([2, 3], 1)
    last_b0, last_b1, last_a0, last_a1 = products(
        (far[1], 1, 0, [(small, got_pass_b0), (large, got_pass_b1)], [large, small]),
        (far[0], 0, 0, [(small, got_pass_a0), (large, got_pass_a1)], [large, small]),
    )
    got_last_b = [swap(v, "dp", far[1]) for v in (last_b0, last_b1)]
    got_last_a = [swap(v, "dp", far[0]) for v in (last_a0, last_a1)]
    got_2a = outer(plus([c2_a, got_m1a], order))
    got_m2b = across(plus([c1_b, got_1b], order))
    *base_b, base_a0, base_a1 = products(
        (0, 1, 0, [(blocks, got_keep_b)], [large, small]),
        (0, 0, 0, [(blocks, got_keep_a)], [large, small]),
        base=(weight, scale),
    )
    base_a = [base_a0, base_a1]
    got_2b = outer(plus([c2_b, got_m1b], order))
    got_m2a = across(plus([c1_a, got_1a], order))
    order += [got_2a, got_m2b]
    outs = ()
    for k in range(2):
        for start, base, last in ((piece, base_b, got_last_b), (0, base_a, got_last_a)):
            column = start + k * large * bn
            outs = update(base[k], last[k], swag_mean, swag_square, blend, column, bn, scale, outs, order)
    input_grad = plus_side_by_side([[c3_a, got_2a, got_m2a], [c3_b, got_2b, got_m2b]], order)
    return (input_grad, *outs)


def solution(mesh):
    in_specs = (
        P("dp", "row"),
        P(("dp", "row"), "col"),
        P(("dp", "row"), "col"),
        P("row", "col"),
        P("dp", "row", "col"),
        P("dp", "row", "col"),
        P(),
        P("dp", "row"),
    )
    out_specs = (
        P(("dp", "col"), "row"),
        P("dp", "row", "col"),
        P("dp", "row", "col"),
        P("dp", "row", "col"),
    )
    scheduled = dict(mesh.shape) == {"dp": 4, "row": 2, "col": 4}
    return jax.shard_map(
        body if scheduled else plain_body, mesh=mesh, in_specs=in_specs, out_specs=out_specs, check_vma=False
    )
```

```python
import jax
import jax.numpy as jnp
from jax import lax
from jax.experimental import pallas as pl
from jax.experimental.pallas import tpu as pltpu
from jax.sharding import PartitionSpec as P

D = 6144


learning_rate = 0.5
VMEM_LIMIT = 24 * 1024 * 1024
LANES = 128
TOKEN = (8, LANES)


def gelu_slope(values):
    normal_cdf = 0.5 * (1.0 + lax.erf(values * 0.7071067811865476))
    density = jnp.exp(-0.5 * values * values) * 0.3989422804014327
    return normal_cdf + values * density


def times_slope(out_grad, pre_act):
    return (out_grad.astype(jnp.float32) * gelu_slope(pre_act.astype(jnp.float32))).astype(jnp.bfloat16)


def dot(a, b, dims):
    return lax.dot_general(a, b, (dims, ((), ())), preferred_element_type=jnp.float32)


def params(limit=VMEM_LIMIT):
    return pltpu.CompilerParams(dimension_semantics=("arbitrary",), vmem_limit_bytes=limit)


def anywhere(arrays):
    return [pl.BlockSpec(memory_space=pl.ANY)] * len(arrays)


def block_width(width, most):
    return max(b for b in range(LANES, min(width, most) + 1, LANES) if width % b == 0)


def block_rows(rows, most):
    return max(b for b in range(16, min(rows, most) + 1, 16) if rows % b == 0)


def cost(flops, bytes_accessed):
    return pl.CostEstimate(flops=flops, bytes_accessed=bytes_accessed, transcendentals=0)


def held(array):
    return pltpu.with_memory_space_constraint(array, pltpu.HBM)


def clipped(first, count):
    return lambda j, ids: (0, jnp.clip(j - first, 0, count - 1))


def weight_product(inputs, mine, theirs, ids, share, bn, jobs, order, base=None):
    half = mine[0].shape[0]
    begins, steps = [], 0
    for job in jobs:
        begins.append(steps)
        steps += sum(job[4])
    kind = jnp.bfloat16 if base is None else jnp.float32

    def bits_at(j):
        bits = jobs[0][0]
        for begin, job in zip(begins[1:], jobs[1:]):
            bits = jnp.where(j >= begin, job[0], bits)
        return bits

    operands = [inputs, inputs]
    in_specs = [
        pl.BlockSpec((half, share), lambda j, ids: (ids[1], ids[0] ^ bits_at(j))),
        pl.BlockSpec((half, share), lambda j, ids: (1 - ids[1], ids[0] ^ bits_at(j))),
    ]
    out_specs, out_shape, plans = [], [], []
    for begin, (_, piece, first, received, outs) in zip(begins, jobs):
        count = sum(outs)

        def column(j, ids, begin=begin, first=first, count=count):
            return (0, first + jnp.clip(j - begin, 0, count - 1))

        grads = (len(operands), len(operands) + 1)
        operands += [mine[piece], theirs[piece]]
        in_specs += [pl.BlockSpec((half, bn), column)] * 2
        adds, at = [], begin
        for blocks, array in received:
            adds.append((at, at + blocks, len(operands)))
            operands.append(array)
            in_specs.append(pl.BlockSpec((share, bn), clipped(at, blocks)))
            at += blocks
        old = None
        if base is not None:
            old = len(operands)
            operands.append(held(base[0]))
            place = sum(m.shape[1] for m in mine[:piece]) // bn + first
            in_specs.append(
                pl.BlockSpec(
                    (share, bn),
                    lambda j, ids, begin=begin, place=place, count=count: (ids[0], place + jnp.clip(j - begin, 0, count - 1)),
                )
            )
        written, at = [], begin
        for blocks in outs:
            written.append((at, at + blocks, len(out_specs)))
            out_specs.append(pl.BlockSpec((share, bn), clipped(at, blocks)))
            out_shape.append(jax.ShapeDtypeStruct((share, blocks * bn), kind))
            at += blocks
        plans.append((begin, begin + count, grads, adds, old, written))

    def kernel(ids_ref, *refs):
        outs, token = refs[-1 - len(out_specs) : -1], refs[-1]
        step = pl.program_id(0)
        token[...] = jnp.zeros_like(token)
        for begin, end, grads, adds, old, written in plans:

            @pl.when((step >= begin) & (step < end))
            def _():
                result = sum(dot(refs[k][...], refs[g][...], ((0,), (0,))) for k, g in enumerate(grads))
                if adds:
                    more = refs[adds[0][2]][...]
                    for since, _, index in adds[1:]:
                        more = jnp.where(step >= since, refs[index][...], more)
                    result = result + more.astype(jnp.float32)
                if old is not None:
                    result = refs[old][...].astype(jnp.float32) - base[1] * result
                for since, until, index in written:

                    @pl.when((step >= since) & (step < until))
                    def _():
                        outs[index][...] = result.astype(kind)

    *arrays, token = pl.pallas_call(
        kernel,
        grid_spec=pltpu.PrefetchScalarGridSpec(
            num_scalar_prefetch=1,
            grid=(steps,),
            in_specs=in_specs + anywhere(order),
            out_specs=out_specs + [pl.BlockSpec(TOKEN, lambda j, ids: (0, 0))],
        ),
        out_shape=out_shape + [jax.ShapeDtypeStruct(TOKEN, jnp.float32)],
        compiler_params=params(),
        cost_estimate=cost(4 * half * share * bn * steps, 2 * steps * bn * (2 * half + share)),
        name="weight_product",
    )(ids, *operands, *order)
    order[:] = [token]
    return arrays


def chunk_of(turn, place, places):
    above = jnp.where(turn < places - 1 - place, places - 1 - turn, turn - (places - 1 - place))
    below = jnp.where(turn < place, turn, places - 1 - (turn - place))
    return jnp.where(turn == places - 1, place, jnp.where(2 * place < places, above, below))


def input_product(weight, mine, theirs, ids, turns, places, first, wide, multiplier, order):
    hidden = weight.shape[1]
    per_half = places // 2
    rows = mine[0].shape[0] // per_half
    bn = block_width(wide, 512)
    steps = wide // bn
    count = len(mine)

    def kernel(ids_ref, w, *rest):
        own, other = rest[:count], rest[count : 2 * count]
        (token, lhs, sem), outs = rest[-3:], rest[-3 - len(turns) : -3]

        @pl.when(pl.program_id(0) == 0)
        def _():
            token[...] = jnp.zeros_like(token)
            copies = []
            for k, turn in enumerate(turns):
                chunk = chunk_of(turn, ids_ref[2], places)
                here = chunk // per_half == ids_ref[1]
                at = 0
                for g in range(count):
                    columns = own[g].shape[1]
                    rows_at = pl.ds(pl.multiple_of((chunk % per_half) * rows, rows), rows)
                    target = lhs.at[pl.ds(k * rows, rows), pl.ds(at, columns)]
                    near = pltpu.make_async_copy(own[g].at[rows_at, :], target, sem.at[k, g])
                    far = pltpu.make_async_copy(other[g].at[rows_at, :], target, sem.at[k, g])
                    pl.when(here)(near.start)
                    pl.when(jnp.logical_not(here))(far.start)
                    copies.append(near)
                    at += columns
            for copy in copies:
                copy.wait()

        result = (dot(lhs[...], w[...], ((1,), (1,))) * multiplier).astype(jnp.bfloat16)
        for k, out in enumerate(outs):
            out[...] = result[k * rows : (k + 1) * rows]

    *arrays, token = pl.pallas_call(
        kernel,
        grid_spec=pltpu.PrefetchScalarGridSpec(
            num_scalar_prefetch=1,
            grid=(steps,),
            in_specs=[pl.BlockSpec((bn, hidden), lambda j, ids: (first // bn + j, 0))]
            + anywhere(mine)
            + anywhere(theirs)
            + anywhere(order),
            out_specs=[pl.BlockSpec((rows, bn), lambda j, ids: (0, j))] * len(turns)
            + [pl.BlockSpec(TOKEN, lambda j, ids: (0, 0))],
            scratch_shapes=[
                pltpu.VMEM((len(turns) * rows, hidden), jnp.bfloat16),
                pltpu.SemaphoreType.DMA((len(turns), count)),
            ],
        ),
        out_shape=[jax.ShapeDtypeStruct((rows, wide), jnp.bfloat16)] * len(turns)
        + [jax.ShapeDtypeStruct(TOKEN, jnp.float32)],
        compiler_params=params(),
        cost_estimate=cost(
            2 * len(turns) * rows * wide * hidden, 2 * (wide * hidden + len(turns) * rows * (hidden + wide))
        ),
        name="input_product",
    )(ids, held(weight), *mine, *theirs, *order)
    order[:] = [token]
    return arrays


def staged(arrays, pieces, order):
    share = arrays[0].shape[1]

    def kernel(*refs):
        sem = refs[-1]
        outs, token = refs[-2 - len(arrays) * len(pieces) : -2], refs[-2]
        token[...] = jnp.zeros_like(token)
        copies = []
        for k, (start, width) in enumerate(pieces):
            for g in range(len(arrays)):
                at = k * len(arrays) + g
                source = refs[g].at[0, :, pl.ds(start, width)]
                copies.append(pltpu.make_async_copy(source, outs[at], sem.at[at]))
        for copy in copies:
            copy.start()
        for copy in copies:
            copy.wait()

    count = len(arrays) * len(pieces)
    *outs, token = pl.pallas_call(
        kernel,
        in_specs=anywhere(arrays) + anywhere(order),
        out_specs=anywhere(range(count)) + [pl.BlockSpec(memory_space=pltpu.VMEM)],
        out_shape=[pltpu.VMEM((share, width), jnp.float32) for _, width in pieces for _ in arrays]
        + [jax.ShapeDtypeStruct(TOKEN, jnp.float32)],
        scratch_shapes=[pltpu.SemaphoreType.DMA((count,))],
        compiler_params=pltpu.CompilerParams(vmem_limit_bytes=VMEM_LIMIT // 8),
        cost_estimate=cost(0, sum(8 * share * width for _, width in pieces) * len(arrays)),
        name="staged",
    )(*(held(a) for a in arrays), *order)
    order[:] = [token]
    return [outs[k : k + len(arrays)] for k in range(0, count, len(arrays))]


def update(base, last, mean, square, whole, blend, column, bn, scale, before, order):
    share, width = base.shape
    rows = block_rows(share, 256)
    across, place = width // bn, column // bn

    def kernel(old, arrived, m, s, b, *rest):
        new_w, new_m, new_s, token = rest[-4:]
        token[...] = jnp.zeros_like(token)
        stepped = old[...] - scale * arrived[...].astype(jnp.float32)
        new_w[0] = stepped
        new_m[0] = m[...] + b[...] * (stepped - m[...])
        new_s[0] = s[...] + b[...] * (stepped * stepped - s[...])

    moment = pl.BlockSpec((1, rows, bn), lambda i: (0, i // across, place + i % across))
    block = pl.BlockSpec((rows, bn), lambda i: (i // across, i % across))
    *outs, token = pl.pallas_call(
        kernel,
        grid=(share // rows * across,),
        in_specs=[block] * 4 + [pl.BlockSpec((rows, 1), lambda i: (i // across, 0))] + anywhere(before) + anywhere(order),
        out_specs=[moment] * 3 + [pl.BlockSpec(TOKEN, lambda i: (0, 0))],
        out_shape=[jax.ShapeDtypeStruct(whole, jnp.float32)] * 3 + [jax.ShapeDtypeStruct(TOKEN, jnp.float32)],
        input_output_aliases={5 + k: k for k in range(len(before))},
        compiler_params=params(VMEM_LIMIT // 2),
        cost_estimate=cost(10 * share * width, share * width * 26),
        name="update",
    )(base, last, *(pltpu.with_memory_space_constraint(a, pltpu.VMEM) for a in (mean, square)), blend, *before, *order)
    order[:] = [token]
    return outs


def plain_body(inputs, pre_act, out_grad, weight, swag_mean, swag_square, snapshots, update_flag):
    row_width = weight.shape[0]
    groups = lax.axis_size("dp")
    share_rows = row_width // groups
    multiplier = 1.0 / D**0.5
    local_grad = times_slope(out_grad, pre_act)
    portion = lax.all_gather(local_grad, "row", axis=0, tiled=True)
    grad_acc = dot(inputs, portion, ((0,), (0,)))
    term_rows = dot(portion, weight, ((1,), (1,))) * multiplier
    input_grad = lax.psum_scatter(term_rows.astype(jnp.bfloat16), "col", scatter_dimension=0, tiled=True)
    share = lax.psum_scatter(grad_acc.astype(jnp.bfloat16), "dp", scatter_dimension=0, tiled=True).astype(jnp.float32)
    own_rows = lax.dynamic_slice_in_dim(weight, lax.axis_index("dp") * share_rows, share_rows, 0).astype(jnp.float32)
    total_tokens = inputs.shape[0] * groups
    stepped = own_rows - learning_rate * (share / total_tokens**0.5)
    blend = update_flag[0].astype(jnp.float32)[:, None] / (snapshots[0].astype(jnp.float32) + 1.0)
    mean_new = swag_mean[0] + blend * (stepped - swag_mean[0])
    square_new = swag_square[0] + blend * (stepped * stepped - swag_square[0])
    return (input_grad, stepped[None], mean_new[None], square_new[None])


def plus(terms, order, beside=()):
    rows, width = terms[0].shape
    some = block_rows(rows, 96)
    count = len(terms)

    def kernel(*refs):
        out, token = refs[-2:]
        token[...] = jnp.zeros_like(token)
        if not beside:
            out[...] = sum(ref[...].astype(jnp.float32) for ref in refs[:count]).astype(out.dtype)
        at = 0
        for ref in refs[count : count + len(beside)]:
            columns = slice(at, at + ref.shape[1])
            total = sum(term[:, columns].astype(jnp.float32) for term in refs[:count]) + ref[...].astype(jnp.float32)
            out[:, columns] = total.astype(out.dtype)
            at += ref.shape[1]

    def block(array):
        return pl.BlockSpec((some, array.shape[1]), lambda i: (i, 0))

    out, token = pl.pallas_call(
        kernel,
        grid=(rows // some,),
        in_specs=[block(a) for a in (*terms, *beside)] + anywhere(order),
        out_specs=[block(terms[0]), pl.BlockSpec(TOKEN, lambda i: (0, 0))],
        out_shape=[jax.ShapeDtypeStruct((rows, width), jnp.bfloat16), jax.ShapeDtypeStruct(TOKEN, jnp.float32)],
        compiler_params=params(),
        cost_estimate=cost(rows * width * (count + 1), 2 * rows * width * (count + 2)),
        name="plus",
    )(*terms, *beside, *order)
    order[:] = [token]
    return out


def body(inputs, pre_act, out_grad, weight, swag_mean, swag_square, snapshots, update_flag):
    tokens = inputs.shape[0]
    half = pre_act.shape[0]
    width, hidden = weight.shape
    groups, cols = lax.axis_size("dp"), lax.axis_size("col")
    share = width // groups
    multiplier = 1.0 / D**0.5
    scale = learning_rate / (tokens * groups) ** 0.5
    ids = jnp.stack([lax.axis_index(axis) for axis in ("dp", "row", "col")]).astype(jnp.int32)

    def swap(value, axis, bit):
        return lax.ppermute(value, axis, [(i, i ^ bit) for i in range(lax.axis_size(axis))])

    piece = hidden // 2
    first = times_slope(out_grad[:, :piece], pre_act[:, :piece])
    rest = lax.optimization_barrier((out_grad, pre_act, first))
    second = times_slope(rest[0][:, piece:], rest[1][:, piece:])
    mine = [first, second]
    theirs = [swap(value, "row", 1) for value in mine]
    blend = update_flag[0].astype(jnp.float32)[:, None] / (snapshots[0].astype(jnp.float32) + 1.0)

    order = []
    bn = block_width(piece, 512)
    blocks = piece // bn
    small = max(1, blocks // 3)
    large = blocks - small

    def products(*jobs, base=None, streamed=False):
        return weight_product(held(inputs) if streamed else inputs, mine, theirs, ids, share, bn, jobs, order, base)

    part = width // 2

    def chunks(turns, first=0, wide=width):
        return input_product(weight, mine, theirs, ids, turns, cols, first, wide, multiplier, order)

    near, far = (1, 2), (2, 1)
    middle = ((1, 2), (2, 1))

    def outer(value):
        return swap(value, "col", 1)

    def across(value):
        return lax.ppermute(value, "col", middle)

    (pass_a0,) = products((3, 0, 0, [], [small]), streamed=True)
    got_pass_a0 = swap(pass_a0, "dp", near[0])
    (c0_a,) = chunks([0], 0, part)
    got_0a = outer(c0_a)
    (pass_b0,) = products((3, 1, 0, [], [small]), streamed=True)
    got_pass_b0 = swap(pass_b0, "dp", near[1])
    pass_a1, pass_b1 = products((3, 0, small, [], [large]), (3, 1, small, [], [large]))
    got_pass_a1, got_pass_b1 = swap(pass_a1, "dp", near[0]), swap(pass_b1, "dp", near[1])
    order += [got_pass_a0]
    (c0_b,) = chunks([0], part, part)
    got_0b = outer(c0_b)
    keep_a, keep_b = products((near[0], 0, 0, [], [blocks]), (near[1], 1, 0, [], [blocks]))
    got_keep_a, got_keep_b = swap(keep_a, "dp", near[0]), swap(keep_b, "dp", near[1])
    order += [got_pass_b0]
    got_m1a = across(plus([c0_a, got_0a], order))
    (c1,) = chunks([1])
    got_1 = outer(c1)
    order += [got_pass_a1, got_pass_b1]
    got_m1b = across(plus([c0_b, got_0b], order))
    order += [got_m1a]
    c2, c3 = chunks([2, 3])
    last_b, last_a = products(
        (far[1], 1, 0, [(small, got_pass_b0), (large, got_pass_b1)], [blocks]),
        (far[0], 0, 0, [(small, got_pass_a0), (large, got_pass_a1)], [blocks]),
    )
    got_last_b, got_last_a = swap(last_b, "dp", far[1]), swap(last_a, "dp", far[0])
    got_2 = outer(plus([c2], order, beside=[got_m1a, got_m1b]))
    order += [got_keep_a, got_keep_b]
    got_m2 = across(plus([c1, got_1], order))
    base_b, base_a = products(
        (0, 1, 0, [(blocks, got_keep_b)], [blocks]), (0, 0, 0, [(blocks, got_keep_a)], [blocks]), base=(weight, scale)
    )
    (mean_b, square_b), (mean_a, square_a) = staged((swag_mean, swag_square), ((piece, piece), (0, piece)), order)
    outs = ()
    outs = update(base_b, got_last_b, mean_b, square_b, swag_mean.shape, blend, piece, bn, scale, outs, order)
    outs = update(base_a, got_last_a, mean_a, square_a, swag_mean.shape, blend, 0, bn, scale, outs, order)
    input_grad = plus([c3, got_2, got_m2], order)
    return (input_grad, *outs)


def solution(mesh):
    in_specs = (
        P("dp", "row"),
        P(("dp", "row"), "col"),
        P(("dp", "row"), "col"),
        P("row", "col"),
        P("dp", "row", "col"),
        P("dp", "row", "col"),
        P(),
        P("dp", "row"),
    )
    out_specs = (
        P(("dp", "col"), "row"),
        P("dp", "row", "col"),
        P("dp", "row", "col"),
        P("dp", "row", "col"),
    )
    scheduled = dict(mesh.shape) == {"dp": 4, "row": 2, "col": 4}
    return jax.shard_map(
        body if scheduled else plain_body, mesh=mesh, in_specs=in_specs, out_specs=out_specs, check_vma=False
    )
```

```python
import jax
import jax.numpy as jnp
from jax import lax
from jax.experimental import pallas as pl
from jax.experimental.pallas import tpu as pltpu
from jax.sharding import PartitionSpec as P

D = 6144


learning_rate = 0.5
VMEM_LIMIT = 24 * 1024 * 1024
LANES = 128
TOKEN = (8, LANES)


def gelu_slope(values):
    normal_cdf = 0.5 * (1.0 + lax.erf(values * 0.7071067811865476))
    density = jnp.exp(-0.5 * values * values) * 0.3989422804014327
    return normal_cdf + values * density


def times_slope(out_grad, pre_act):
    return (out_grad.astype(jnp.float32) * gelu_slope(pre_act.astype(jnp.float32))).astype(jnp.bfloat16)


def dot(a, b, dims):
    return lax.dot_general(a, b, (dims, ((), ())), preferred_element_type=jnp.float32)


def params(limit=VMEM_LIMIT):
    return pltpu.CompilerParams(dimension_semantics=("arbitrary",), vmem_limit_bytes=limit)


def anywhere(arrays):
    return [pl.BlockSpec(memory_space=pl.ANY)] * len(arrays)


def block_width(width, most):
    return max(b for b in range(LANES, min(width, most) + 1, LANES) if width % b == 0)


def block_rows(rows, most):
    return max(b for b in range(16, min(rows, most) + 1, 16) if rows % b == 0)


def cost(flops, bytes_accessed):
    return pl.CostEstimate(flops=flops, bytes_accessed=bytes_accessed, transcendentals=0)


def held(array):
    return pltpu.with_memory_space_constraint(array, pltpu.HBM)


def clipped(first, count):
    return lambda j, ids: (0, jnp.clip(j - first, 0, count - 1))


def weight_product(inputs, mine, theirs, ids, share, bn, jobs, order, base=None):
    half = mine[0].shape[0]
    begins, steps = [], 0
    for job in jobs:
        begins.append(steps)
        steps += sum(job[4])
    kind = jnp.bfloat16 if base is None else jnp.float32

    def bits_at(j):
        bits = jobs[0][0]
        for begin, job in zip(begins[1:], jobs[1:]):
            bits = jnp.where(j >= begin, job[0], bits)
        return bits

    operands = [inputs, inputs]
    in_specs = [
        pl.BlockSpec((half, share), lambda j, ids: (ids[1], ids[0] ^ bits_at(j))),
        pl.BlockSpec((half, share), lambda j, ids: (1 - ids[1], ids[0] ^ bits_at(j))),
    ]
    out_specs, out_shape, plans = [], [], []
    for begin, (_, piece, first, received, outs) in zip(begins, jobs):
        count = sum(outs)

        def column(j, ids, begin=begin, first=first, count=count):
            return (0, first + jnp.clip(j - begin, 0, count - 1))

        grads = (len(operands), len(operands) + 1)
        operands += [mine[piece], theirs[piece]]
        in_specs += [pl.BlockSpec((half, bn), column)] * 2
        adds, at = [], begin
        for blocks, array in received:
            adds.append((at, at + blocks, len(operands)))
            operands.append(array)
            in_specs.append(pl.BlockSpec((share, bn), clipped(at, blocks)))
            at += blocks
        old = None
        if base is not None:
            old = len(operands)
            operands.append(held(base[0]))
            place = sum(m.shape[1] for m in mine[:piece]) // bn + first
            in_specs.append(
                pl.BlockSpec(
                    (share, bn),
                    lambda j, ids, begin=begin, place=place, count=count: (ids[0], place + jnp.clip(j - begin, 0, count - 1)),
                )
            )
        written, at = [], begin
        for blocks in outs:
            written.append((at, at + blocks, len(out_specs)))
            out_specs.append(pl.BlockSpec((share, bn), clipped(at, blocks)))
            out_shape.append(jax.ShapeDtypeStruct((share, blocks * bn), kind))
            at += blocks
        plans.append((begin, begin + count, grads, adds, old, written))

    def kernel(ids_ref, *refs):
        outs, token = refs[-1 - len(out_specs) : -1], refs[-1]
        step = pl.program_id(0)
        token[...] = jnp.zeros_like(token)
        for begin, end, grads, adds, old, written in plans:

            @pl.when((step >= begin) & (step < end))
            def _():
                result = sum(dot(refs[k][...], refs[g][...], ((0,), (0,))) for k, g in enumerate(grads))
                if adds:
                    more = refs[adds[0][2]][...]
                    for since, _, index in adds[1:]:
                        more = jnp.where(step >= since, refs[index][...], more)
                    result = result + more.astype(jnp.float32)
                if old is not None:
                    result = refs[old][...].astype(jnp.float32) - base[1] * result
                for since, until, index in written:

                    @pl.when((step >= since) & (step < until))
                    def _():
                        outs[index][...] = result.astype(kind)

    *arrays, token = pl.pallas_call(
        kernel,
        grid_spec=pltpu.PrefetchScalarGridSpec(
            num_scalar_prefetch=1,
            grid=(steps,),
            in_specs=in_specs + anywhere(order),
            out_specs=out_specs + [pl.BlockSpec(TOKEN, lambda j, ids: (0, 0))],
        ),
        out_shape=out_shape + [jax.ShapeDtypeStruct(TOKEN, jnp.float32)],
        compiler_params=params(),
        cost_estimate=cost(4 * half * share * bn * steps, 2 * steps * bn * (2 * half + share)),
        name="weight_product",
    )(ids, *operands, *order)
    order[:] = [token]
    return arrays


def chunk_of(turn, place, places):
    above = jnp.where(turn < places - 1 - place, places - 1 - turn, turn - (places - 1 - place))
    below = jnp.where(turn < place, turn, places - 1 - (turn - place))
    return jnp.where(turn == places - 1, place, jnp.where(2 * place < places, above, below))


def input_product(weight, mine, theirs, ids, turns, places, first, wide, multiplier, order):
    hidden = weight.shape[1]
    per_half = places // 2
    rows = mine[0].shape[0] // per_half
    bn = block_width(wide, 512)
    steps = wide // bn
    count = len(mine)

    def kernel(ids_ref, w, *rest):
        own, other = rest[:count], rest[count : 2 * count]
        (token, lhs, sem), outs = rest[-3:], rest[-3 - len(turns) : -3]

        @pl.when(pl.program_id(0) == 0)
        def _():
            token[...] = jnp.zeros_like(token)
            copies = []
            for k, turn in enumerate(turns):
                chunk = chunk_of(turn, ids_ref[2], places)
                here = chunk // per_half == ids_ref[1]
                at = 0
                for g in range(count):
                    columns = own[g].shape[1]
                    rows_at = pl.ds(pl.multiple_of((chunk % per_half) * rows, rows), rows)
                    target = lhs.at[pl.ds(k * rows, rows), pl.ds(at, columns)]
                    near = pltpu.make_async_copy(own[g].at[rows_at, :], target, sem.at[k, g])
                    far = pltpu.make_async_copy(other[g].at[rows_at, :], target, sem.at[k, g])
                    pl.when(here)(near.start)
                    pl.when(jnp.logical_not(here))(far.start)
                    copies.append(near)
                    at += columns
            for copy in copies:
                copy.wait()

        result = (dot(lhs[...], w[...], ((1,), (1,))) * multiplier).astype(jnp.bfloat16)
        for k, out in enumerate(outs):
            out[...] = result[k * rows : (k + 1) * rows]

    *arrays, token = pl.pallas_call(
        kernel,
        grid_spec=pltpu.PrefetchScalarGridSpec(
            num_scalar_prefetch=1,
            grid=(steps,),
            in_specs=[pl.BlockSpec((bn, hidden), lambda j, ids: (first // bn + j, 0))]
            + anywhere(mine)
            + anywhere(theirs)
            + anywhere(order),
            out_specs=[pl.BlockSpec((rows, bn), lambda j, ids: (0, j))] * len(turns)
            + [pl.BlockSpec(TOKEN, lambda j, ids: (0, 0))],
            scratch_shapes=[
                pltpu.VMEM((len(turns) * rows, hidden), jnp.bfloat16),
                pltpu.SemaphoreType.DMA((len(turns), count)),
            ],
        ),
        out_shape=[jax.ShapeDtypeStruct((rows, wide), jnp.bfloat16)] * len(turns)
        + [jax.ShapeDtypeStruct(TOKEN, jnp.float32)],
        compiler_params=params(),
        cost_estimate=cost(
            2 * len(turns) * rows * wide * hidden, 2 * (wide * hidden + len(turns) * rows * (hidden + wide))
        ),
        name="input_product",
    )(ids, held(weight), *mine, *theirs, *order)
    order[:] = [token]
    return arrays


def staged(arrays, pieces, order):
    share = arrays[0].shape[1]

    def kernel(*refs):
        sem = refs[-1]
        outs, token = refs[-2 - len(arrays) * len(pieces) : -2], refs[-2]
        token[...] = jnp.zeros_like(token)
        copies = []
        for k, (start, width) in enumerate(pieces):
            for g in range(len(arrays)):
                at = k * len(arrays) + g
                source = refs[g].at[0, :, pl.ds(start, width)]
                copies.append(pltpu.make_async_copy(source, outs[at], sem.at[at]))
        for copy in copies:
            copy.start()
        for copy in copies:
            copy.wait()

    count = len(arrays) * len(pieces)
    *outs, token = pl.pallas_call(
        kernel,
        in_specs=anywhere(arrays) + anywhere(order),
        out_specs=anywhere(range(count)) + [pl.BlockSpec(memory_space=pltpu.VMEM)],
        out_shape=[pltpu.VMEM((share, width), jnp.float32) for _, width in pieces for _ in arrays]
        + [jax.ShapeDtypeStruct(TOKEN, jnp.float32)],
        scratch_shapes=[pltpu.SemaphoreType.DMA((count,))],
        compiler_params=pltpu.CompilerParams(vmem_limit_bytes=VMEM_LIMIT // 8),
        cost_estimate=cost(0, sum(8 * share * width for _, width in pieces) * len(arrays)),
        name="staged",
    )(*(held(a) for a in arrays), *order)
    order[:] = [token]
    return [outs[k : k + len(arrays)] for k in range(0, count, len(arrays))]


def update(base, last, mean, square, whole, blend, column, bn, scale, before, order):
    share, width = base.shape
    rows = block_rows(share, 768)
    across, place = width // bn, column // bn

    def kernel(old, arrived, m, s, b, *rest):
        new_w, new_m, new_s, token = rest[-4:]
        token[...] = jnp.zeros_like(token)
        stepped = old[...] - scale * arrived[...].astype(jnp.float32)
        new_w[0] = stepped
        new_m[0] = m[...] + b[...] * (stepped - m[...])
        new_s[0] = s[...] + b[...] * (stepped * stepped - s[...])

    moment = pl.BlockSpec((1, rows, bn), lambda i: (0, i // across, place + i % across))
    block = pl.BlockSpec((rows, bn), lambda i: (i // across, i % across))
    *outs, token = pl.pallas_call(
        kernel,
        grid=(share // rows * across,),
        in_specs=[block] * 4 + [pl.BlockSpec((rows, 1), lambda i: (i // across, 0))] + anywhere(before) + anywhere(order),
        out_specs=[moment] * 3 + [pl.BlockSpec(TOKEN, lambda i: (0, 0))],
        out_shape=[jax.ShapeDtypeStruct(whole, jnp.float32)] * 3 + [jax.ShapeDtypeStruct(TOKEN, jnp.float32)],
        input_output_aliases={5 + k: k for k in range(len(before))},
        compiler_params=params(),
        cost_estimate=cost(10 * share * width, share * width * 26),
        name="update",
    )(base, last, *(pltpu.with_memory_space_constraint(a, pltpu.VMEM) for a in (mean, square)), blend, *before, *order)
    order[:] = [token]
    return outs


def plain_body(inputs, pre_act, out_grad, weight, swag_mean, swag_square, snapshots, update_flag):
    row_width = weight.shape[0]
    groups = lax.axis_size("dp")
    share_rows = row_width // groups
    multiplier = 1.0 / D**0.5
    local_grad = times_slope(out_grad, pre_act)
    portion = lax.all_gather(local_grad, "row", axis=0, tiled=True)
    grad_acc = dot(inputs, portion, ((0,), (0,)))
    term_rows = dot(portion, weight, ((1,), (1,))) * multiplier
    input_grad = lax.psum_scatter(term_rows.astype(jnp.bfloat16), "col", scatter_dimension=0, tiled=True)
    share = lax.psum_scatter(grad_acc.astype(jnp.bfloat16), "dp", scatter_dimension=0, tiled=True).astype(jnp.float32)
    own_rows = lax.dynamic_slice_in_dim(weight, lax.axis_index("dp") * share_rows, share_rows, 0).astype(jnp.float32)
    total_tokens = inputs.shape[0] * groups
    stepped = own_rows - learning_rate * (share / total_tokens**0.5)
    blend = update_flag[0].astype(jnp.float32)[:, None] / (snapshots[0].astype(jnp.float32) + 1.0)
    mean_new = swag_mean[0] + blend * (stepped - swag_mean[0])
    square_new = swag_square[0] + blend * (stepped * stepped - swag_square[0])
    return (input_grad, stepped[None], mean_new[None], square_new[None])


def plus(terms, order, beside=()):
    rows, width = terms[0].shape
    some = block_rows(rows, 192)
    count = len(terms)

    def kernel(*refs):
        out, token = refs[-2:]
        token[...] = jnp.zeros_like(token)
        if not beside:
            out[...] = sum(ref[...].astype(jnp.float32) for ref in refs[:count]).astype(out.dtype)
        at = 0
        for ref in refs[count : count + len(beside)]:
            columns = slice(at, at + ref.shape[1])
            total = sum(term[:, columns].astype(jnp.float32) for term in refs[:count]) + ref[...].astype(jnp.float32)
            out[:, columns] = total.astype(out.dtype)
            at += ref.shape[1]

    def block(array):
        return pl.BlockSpec((some, array.shape[1]), lambda i: (i, 0))

    out, token = pl.pallas_call(
        kernel,
        grid=(rows // some,),
        in_specs=[block(a) for a in (*terms, *beside)] + anywhere(order),
        out_specs=[block(terms[0]), pl.BlockSpec(TOKEN, lambda i: (0, 0))],
        out_shape=[jax.ShapeDtypeStruct((rows, width), jnp.bfloat16), jax.ShapeDtypeStruct(TOKEN, jnp.float32)],
        compiler_params=params(),
        cost_estimate=cost(rows * width * (count + 1), 2 * rows * width * (count + 2)),
        name="plus",
    )(*terms, *beside, *order)
    order[:] = [token]
    return out


def body(inputs, pre_act, out_grad, weight, swag_mean, swag_square, snapshots, update_flag):
    tokens = inputs.shape[0]
    half = pre_act.shape[0]
    width, hidden = weight.shape
    groups, cols = lax.axis_size("dp"), lax.axis_size("col")
    share = width // groups
    multiplier = 1.0 / D**0.5
    scale = learning_rate / (tokens * groups) ** 0.5
    ids = jnp.stack([lax.axis_index(axis) for axis in ("dp", "row", "col")]).astype(jnp.int32)

    def swap(value, axis, bit):
        return lax.ppermute(value, axis, [(i, i ^ bit) for i in range(lax.axis_size(axis))])

    piece = hidden // 2
    first = times_slope(out_grad[:, :piece], pre_act[:, :piece])
    rest = lax.optimization_barrier((out_grad, pre_act, first))
    second = times_slope(rest[0][:, piece:], rest[1][:, piece:])
    mine = [first, second]
    theirs = [swap(value, "row", 1) for value in mine]
    blend = update_flag[0].astype(jnp.float32)[:, None] / (snapshots[0].astype(jnp.float32) + 1.0)

    order = []
    bn = block_width(piece, 512)
    blocks = piece // bn
    small = max(1, blocks // 3)
    large = blocks - small

    def products(*jobs, base=None, streamed=False, late=False):
        rows = held(inputs) if streamed else inputs
        sides = [[held(a) for a in side] if late else side for side in (mine, theirs)]
        return weight_product(rows, *sides, ids, share, bn, jobs, order, base)

    part = width // 2

    def chunks(turns, first=0, wide=width):
        return input_product(weight, mine, theirs, ids, turns, cols, first, wide, multiplier, order)

    near, far = (1, 2), (2, 1)
    middle = ((1, 2), (2, 1))

    def outer(value):
        return swap(value, "col", 1)

    def across(value):
        return lax.ppermute(value, "col", middle)

    (pass_a0,) = products((3, 0, 0, [], [small]), streamed=True)
    got_pass_a0 = swap(pass_a0, "dp", near[0])
    (c0_a,) = chunks([0], 0, part)
    got_0a = outer(c0_a)
    (pass_b0,) = products((3, 1, 0, [], [small]), streamed=True)
    got_pass_b0 = swap(pass_b0, "dp", near[1])
    pass_a1, pass_b1 = products((3, 0, small, [], [large]), (3, 1, small, [], [large]))
    got_pass_a1, got_pass_b1 = swap(pass_a1, "dp", near[0]), swap(pass_b1, "dp", near[1])
    order += [got_pass_a0]
    (c0_b,) = chunks([0], part, part)
    got_0b = outer(c0_b)
    keep_a, keep_b = products((near[0], 0, 0, [], [blocks]), (near[1], 1, 0, [], [blocks]), late=True)
    got_keep_a, got_keep_b = swap(keep_a, "dp", near[0]), swap(keep_b, "dp", near[1])
    order += [got_pass_b0]
    got_m1a = across(plus([c0_a, got_0a], order))
    (c1,) = chunks([1])
    got_1 = outer(c1)
    order += [got_pass_a1, got_pass_b1]
    got_m1b = across(plus([c0_b, got_0b], order))
    order += [got_m1a]
    c2, c3 = chunks([2, 3])
    last_b, last_a = products(
        (far[1], 1, 0, [(small, got_pass_b0), (large, got_pass_b1)], [blocks]),
        (far[0], 0, 0, [(small, got_pass_a0), (large, got_pass_a1)], [blocks]),
        late=True,
    )
    got_last_b, got_last_a = swap(last_b, "dp", far[1]), swap(last_a, "dp", far[0])
    got_2 = outer(plus([c2], order, beside=[got_m1a, got_m1b]))
    order += [got_keep_a, got_keep_b]
    got_m2 = across(plus([c1, got_1], order))
    base_b, base_a = products(
        (0, 1, 0, [(blocks, got_keep_b)], [blocks]), (0, 0, 0, [(blocks, got_keep_a)], [blocks]), base=(weight, scale), late=True
    )
    (mean_b, square_b), (mean_a, square_a) = staged((swag_mean, swag_square), ((piece, piece), (0, piece)), order)
    outs = ()
    outs = update(base_b, got_last_b, mean_b, square_b, swag_mean.shape, blend, piece, bn, scale, outs, order)
    outs = update(base_a, got_last_a, mean_a, square_a, swag_mean.shape, blend, 0, bn, scale, outs, order)
    input_grad = plus([c3, got_2, got_m2], order)
    return (input_grad, *outs)


def solution(mesh):
    in_specs = (
        P("dp", "row"),
        P(("dp", "row"), "col"),
        P(("dp", "row"), "col"),
        P("row", "col"),
        P("dp", "row", "col"),
        P("dp", "row", "col"),
        P(),
        P("dp", "row"),
    )
    out_specs = (
        P(("dp", "col"), "row"),
        P("dp", "row", "col"),
        P("dp", "row", "col"),
        P("dp", "row", "col"),
    )
    scheduled = dict(mesh.shape) == {"dp": 4, "row": 2, "col": 4}
    return jax.shard_map(
        body if scheduled else plain_body, mesh=mesh, in_specs=in_specs, out_specs=out_specs, check_vma=False
    )
```
